256 devices in a mesh: frames: 32 (over y, z), heads: 8 (over x, core).
Axes of the slice: x: 4, y: 4, z: 8, core: 2. Of those that a mesh axis runs over, the one named last changes fastest.
Arguments:
- queries: bfloat16 [36864, 3072], P(('frames', 'heads')), may hold values from -8 to 8
- keys: bfloat16 [36864, 3072], P(('frames', 'heads')), may hold values from -8 to 8
- values: bfloat16 [36864, 3072], P(('frames', 'heads')), may hold values from -6 to 6
- out_grad: bfloat16 [36864, 3072], P(('frames', 'heads')), may hold values from -6 to 6
- windows: int32 [96, 5], replicated, may hold values from -1 to 95, as said below
Outputs:
- query_grad: bfloat16 [36864, 3072], P(('frames', 'heads'))
- key_grad: bfloat16 [36864, 3072], P(('frames', 'heads'))
- value_grad: bfloat16 [36864, 3072], P(('frames', 'heads'))
The draws below stay inside these ranges and needn't reach their ends.
Inputs may be any that keep to these rules, and one draw needn't show every extreme that they name: Row t of windows starts with t itself; its other 4 entries are distinct tiles other than t whose time row (tile index // 3) differs from that of t by at most one, or -1 for an absent entry.
All inputs are finite; a program needn't handle non-finite values.
Results may differ from the reference program's by a relative error of at most 0.012.
The reference program's roundings to bfloat16 on the way (of `probs` and `score_grad`) count: a program that leaves them out, or rounds other values in their place, can miss the bound.
Values may be sent and summed in bfloat16 or wider, within the bound.
No kernel may reach another device: no remote copies, remote signals or barrier semaphores. Data moves between devices by JAX's collectives and lax.ppermute only.
A program may use at most 256 MiB of HBM per device.

```python
import jax
import jax.numpy as jnp
from jax import lax

HEADS = 24
HEAD_DIM = 128
TILE = 384
WIN = 5
TILES_DEV = 3
NT = 96
TOKENS = 36864


def draw_queries(key, part):
    key = jax.random.fold_in(key, 3)
    field_shape = (TOKENS, HEADS * HEAD_DIM)
    field = jax.random.truncated_normal(key, -4.0, 4.0, field_shape, jnp.float32)
    return field.astype(jnp.bfloat16)


def draw_keys(key, part):
    key = jax.random.fold_in(key, 5)
    field_shape = (TOKENS, HEADS * HEAD_DIM)
    field = jax.random.truncated_normal(key, -4.0, 4.0, field_shape, jnp.float32)
    return field.astype(jnp.bfloat16)


def draw_windows(key, part):
    key = jax.random.fold_in(key, 11)
    candidates = 3 * TILES_DEV

    def one_tile(tile_key, tile):
        time_row = tile // TILES_DEV
        column = tile % TILES_DEV
        order = jax.random.permutation(tile_key, candidates - 1)[:WIN - 1]
        self_place = TILES_DEV + column
        picked = jnp.where(order >= self_place, order + 1, order)
        global_ids = (time_row - 1) * TILES_DEV + picked
        keeping = jax.random.randint(jax.random.fold_in(tile_key, 1), (WIN - 1,), 0, 4) > 0
        inside = (global_ids >= 0) & (global_ids < NT) & keeping
        others = jnp.where(inside, global_ids, -1)
        return jnp.concatenate([tile[None], others]).astype(jnp.int32)
    tile_keys = jax.random.split(key, NT)
    return jax.vmap(one_tile)(tile_keys, jnp.arange(NT, dtype=jnp.int32))


def level_of(own_key, shape, cuts, low, top_value):
    factor_of = 1.0
    for dim, parts in cuts:
        steps = jax.random.uniform(jax.random.fold_in(jax.random.fold_in(own_key, 6), dim), (parts,), jnp.float32, low / len(cuts), top_value / len(cuts))
        factor_of = factor_of * jnp.repeat(jnp.exp(steps), shape[dim] // parts).reshape((-1,) + (1,) * (len(shape) - 1 - dim))
    return factor_of


def noise(stream_key, extent, spread, limit, shards=(), held_as=jnp.bfloat16):
    values = jax.random.normal(stream_key, extent, jnp.float32) * spread
    if len(shards) > 0:
        values = level_of(stream_key, extent, shards, -0.22, 0.18) * values
    return jnp.clip(values, min=-limit, max=limit).astype(held_as)


def setup_inputs(seed: int = 0) -> dict:
    key_of = jax.random.split(jax.random.key(seed), 6)
    queries = draw_queries(jax.random.fold_in(key_of[5], 71), 0)
    keys = draw_keys(jax.random.fold_in(key_of[5], 71), 0)
    values = noise(key_of[2], (TOKENS, HEADS * HEAD_DIM), 1.0, 6.0, ((0, 256),))
    out_grad = noise(key_of[3], (TOKENS, HEADS * HEAD_DIM), 1.0, 6.0, ((0, 256),))
    windows = draw_windows(jax.random.fold_in(key_of[5], 71), 0)
    return dict(queries=queries, keys=keys, values=values, out_grad=out_grad, windows=windows)


def tile_terms(query_tile, grad_tile, key_rows, value_rows, usable, factor):
    query_f = query_tile.astype(jnp.float32)
    grad_f = grad_tile.astype(jnp.float32)
    key_f = key_rows.astype(jnp.float32)
    value_f = value_rows.astype(jnp.float32)
    mask = usable[None, None, :, None]
    scores = jnp.einsum('qhd,wkhd->hqwk', query_f, key_f) * factor
    scores = jnp.where(mask, scores, -1e30)
    row_max = jnp.max(scores, axis=(2, 3))
    row_sum = jnp.sum(jnp.exp(scores - row_max[:, :, None, None]), axis=(2, 3))
    log_sum = row_max + jnp.log(row_sum)
    weights = jnp.where(mask, jnp.exp(scores - log_sum[:, :, None, None]), jnp.float32(0.0))
    probs = lax.optimization_barrier(weights.astype(jnp.bfloat16)).astype(jnp.float32)
    attended = jnp.einsum('hqwk,wkhd->qhd', probs, value_f)
    row_dot = jnp.sum(grad_f * attended, axis=2).T
    prob_grad = jnp.einsum('qhd,wkhd->hqwk', grad_f, value_f)
    score_raw = weights * (prob_grad - row_dot[:, :, None, None])
    score_grad = lax.optimization_barrier(score_raw.astype(jnp.bfloat16)).astype(jnp.float32)
    query_part = jnp.einsum('hqwk,wkhd->qhd', score_grad, key_f) * factor
    key_part = jnp.einsum('hqwk,qhd->wkhd', score_grad, query_f) * factor
    value_part = jnp.einsum('hqwk,qhd->wkhd', probs, grad_f)
    return query_part, key_part, value_part


def reference(queries, keys, values, out_grad, windows):
    tile_total = windows.shape[0]
    tile_shape = (tile_total, TILE, HEADS, HEAD_DIM)
    factor = HEAD_DIM ** -0.5
    query_all = queries.reshape(tile_shape)
    key_all = keys.reshape(tile_shape)
    value_all = values.reshape(tile_shape)
    grad_all = out_grad.reshape(tile_shape)

    def step(carry, members):
        key_acc, value_acc = carry
        query_tile, grad_tile, lists = members
        usable = lists >= 0
        slot_ids = jnp.where(usable, lists, 0).astype(jnp.int32)
        query_part, key_part, value_part = tile_terms(query_tile, grad_tile, key_all[slot_ids], value_all[slot_ids], usable, factor)
        key_acc = key_acc.at[slot_ids].add(key_part)
        value_acc = value_acc.at[slot_ids].add(value_part)
        return (key_acc, value_acc), query_part.astype(jnp.bfloat16)

    zeros = jnp.zeros(tile_shape, jnp.float32)
    (key_acc, value_acc), query_grad = lax.scan(step, (zeros, zeros), (query_all, grad_all, windows))
    width = HEADS * HEAD_DIM
    return (query_grad.reshape(-1, width), key_acc.astype(jnp.bfloat16).reshape(-1, width), value_acc.astype(jnp.bfloat16).reshape(-1, width))
```

```python
import functools

import jax
import jax.numpy as jnp
from jax import lax
from jax.experimental import pallas as pl
from jax.experimental.pallas import tpu as pltpu
from jax.sharding import PartitionSpec as P

HEAD_DIM = 128
TILE = 384
WIN = 5
PAIR = 2 * HEAD_DIM
SUB = 128
SUBS = TILE // SUB
NEG = -1e30
LOG2E = 1.4426950408889634
NT = (((1,), (1,)), ((), ()))
TN = (((0,), (0,)), ((), ()))


def pack_kernel(groups, a_ref, b_ref, out_ref):
    for g in range(groups):
        cols = slice(g * HEAD_DIM, (g + 1) * HEAD_DIM)
        out_ref[g, :, :HEAD_DIM] = a_ref[:, cols]
        out_ref[g, :, HEAD_DIM:] = b_ref[:, cols]


def pack(a, b, chunk, groups):
    rows = a.shape[0]
    block = pl.BlockSpec((rows, groups * HEAD_DIM), lambda i: (0, chunk))
    return pl.pallas_call(
        functools.partial(pack_kernel, groups),
        grid=(1,),
        out_shape=jax.ShapeDtypeStruct((groups, rows, PAIR), a.dtype),
        in_specs=[block, block],
        out_specs=pl.BlockSpec((groups, rows, PAIR), lambda i: (0, 0, 0)),
        cost_estimate=pl.CostEstimate(
            flops=0, bytes_accessed=groups * rows * PAIR * 4, transcendentals=0
        ),
        name="pack",
    )(a, b)


def unpack_kernel(groups, dq_ref, dkv_ref, *refs):
    out_q, out_k, out_v = refs[-3:]
    for g in range(groups):
        cols = slice(g * HEAD_DIM, (g + 1) * HEAD_DIM)
        out_q[:, cols] = dq_ref[g]
        out_k[:, cols] = dkv_ref[g, :, :HEAD_DIM]
        out_v[:, cols] = dkv_ref[g, :, HEAD_DIM:]


def unpack(dq, dkv, before, chunk, chunks):
    groups, rows, _ = dq.shape
    out_block = pl.BlockSpec((rows, groups * HEAD_DIM), lambda i: (0, chunk))
    shape = jax.ShapeDtypeStruct((rows, chunks * groups * HEAD_DIM), dq.dtype)
    return pl.pallas_call(
        functools.partial(unpack_kernel, groups),
        grid=(1,),
        out_shape=[shape] * 3,
        in_specs=[
            pl.BlockSpec(dq.shape, lambda i: (0, 0, 0)),
            pl.BlockSpec(dkv.shape, lambda i: (0, 0, 0)),
        ]
        + [pl.BlockSpec(memory_space=pl.ANY)] * len(before),
        out_specs=[out_block] * 3,
        input_output_aliases={2 + i: i for i in range(len(before))},
        cost_estimate=pl.CostEstimate(
            flops=0, bytes_accessed=groups * rows * HEAD_DIM * 12, transcendentals=0
        ),
        name="unpack",
    )(dq, dkv, *before)


def attend_kernel(
    tiles,
    slot_ref,
    qg_hbm,
    own_hbm,
    prev_hbm,
    next_hbm,
    dq_ref,
    dprev_ref,
    down_ref,
    dnext_ref,
    qg_ref,
    kv_ref,
    acc_ref,
    both_ref,
    score_ref,
    pgrad_ref,
    grad_ref,
    sems,
):
    rows = tiles * TILE
    copies = [
        pltpu.make_async_copy(qg_hbm, qg_ref, sems.at[0]),
        pltpu.make_async_copy(own_hbm, kv_ref.at[pl.ds(rows, rows)], sems.at[1]),
        pltpu.make_async_copy(prev_hbm, kv_ref.at[pl.ds(0, rows)], sems.at[2]),
        pltpu.make_async_copy(next_hbm, kv_ref.at[pl.ds(2 * rows, rows)], sems.at[3]),
    ]
    for copy in copies:
        copy.start()
    acc_ref[...] = jnp.zeros_like(acc_ref)
    both_ref[...] = jnp.zeros_like(both_ref)
    for copy in copies:
        copy.wait()
    factor = HEAD_DIM ** (-0.5)
    scale = factor * LOG2E

    def one_tile(t, carry):
        base = pl.multiple_of(t * TILE, TILE)
        both_ref[:TILE, :HEAD_DIM] = qg_ref[pl.ds(base, TILE), :HEAD_DIM]
        both_ref[TILE:, HEAD_DIM:] = qg_ref[pl.ds(base, TILE), HEAD_DIM:]
        used = [slot_ref[t, j] >= 0 for j in range(WIN)]
        places = [
            pl.multiple_of(jnp.maximum(slot_ref[t, j], 0) * TILE, TILE) for j in range(WIN)
        ]
        both = both_ref[...]
        top = jnp.full((1, TILE), NEG, jnp.float32)
        for j in range(WIN):
            for s in range(SUBS):
                kv = kv_ref[pl.ds(places[j] + s * SUB, SUB), :]
                out = lax.dot_general(kv, both, NT, preferred_element_type=jnp.float32)
                score = out[:, :TILE]
                score_ref[j, s * SUB : (s + 1) * SUB, :] = score
                pgrad_ref[j, s * SUB : (s + 1) * SUB, :] = out[:, TILE:]
                here = jnp.max(score, axis=0, keepdims=True)
                top = jnp.maximum(top, jnp.where(used[j], here, NEG))
        top = top * scale
        total = jnp.zeros((1, TILE), jnp.float32)
        for j in range(WIN):
            shift = jnp.where(used[j], top, -NEG)
            for s in range(SUBS):
                part = slice(s * SUB, (s + 1) * SUB)
                weight = jnp.exp2(score_ref[j, part, :] * scale - shift)
                score_ref[j, part, :] = weight
                total = total + jnp.sum(weight, axis=0, keepdims=True)
        inverse = 1.0 / total
        row_dot = jnp.zeros((1, TILE), jnp.float32)
        for j in range(WIN):
            for s in range(SUBS):
                part = slice(s * SUB, (s + 1) * SUB)
                prob = (score_ref[j, part, :] * inverse).astype(jnp.bfloat16)
                grad_ref[j, part, TILE:] = prob
                row_dot = row_dot + jnp.sum(
                    prob.astype(jnp.float32) * pgrad_ref[j, part, :], axis=0, keepdims=True
                )
        for j in range(WIN):
            for s in range(SUBS):
                part = slice(s * SUB, (s + 1) * SUB)
                weight = score_ref[j, part, :] * inverse
                grad_ref[j, part, :TILE] = (weight * (pgrad_ref[j, part, :] - row_dot)).astype(
                    jnp.bfloat16
                )
        dq = jnp.zeros((TILE, HEAD_DIM), jnp.float32)
        for j in range(WIN):
            place = pl.ds(places[j], TILE)
            acc_ref[place, :] += jnp.dot(
                grad_ref[j], both, preferred_element_type=jnp.float32
            )
            dq = dq + lax.dot_general(
                grad_ref[j, :, :TILE],
                kv_ref[place, :HEAD_DIM],
                TN,
                preferred_element_type=jnp.float32,
            )
        dq_ref[pl.ds(base, TILE), :] = (dq * factor).astype(dq_ref.dtype)
        return carry

    lax.fori_loop(0, tiles, one_tile, 0)
    lanes = lax.broadcasted_iota(jnp.int32, (1, PAIR), 1)
    side = jnp.where(lanes < HEAD_DIM, jnp.float32(factor), jnp.float32(1.0))
    dprev_ref[...] = (acc_ref[:rows, :] * side).astype(dprev_ref.dtype)
    down_ref[...] = acc_ref[rows : 2 * rows, :] * side
    dnext_ref[...] = (acc_ref[2 * rows :, :] * side).astype(dnext_ref.dtype)


def attend(slots, qg, own, prev, after):
    rows = qg.shape[0]
    tiles = rows // TILE
    hbm = pl.BlockSpec(memory_space=pl.ANY)
    vmem = pl.BlockSpec(memory_space=pltpu.VMEM)
    return pl.pallas_call(
        functools.partial(attend_kernel, tiles),
        out_shape=[
            jax.ShapeDtypeStruct((rows, HEAD_DIM), qg.dtype),
            jax.ShapeDtypeStruct((rows, PAIR), qg.dtype),
            jax.ShapeDtypeStruct((rows, PAIR), jnp.float32),
            jax.ShapeDtypeStruct((rows, PAIR), qg.dtype),
        ],
        in_specs=[pl.BlockSpec(memory_space=pltpu.SMEM), hbm, hbm, hbm, hbm],
        out_specs=[vmem] * 4,
        scratch_shapes=[
            pltpu.VMEM((rows, PAIR), qg.dtype),
            pltpu.VMEM((3 * rows, PAIR), qg.dtype),
            pltpu.VMEM((3 * rows, PAIR), jnp.float32),
            pltpu.VMEM((2 * TILE, PAIR), qg.dtype),
            pltpu.VMEM((WIN, TILE, TILE), jnp.float32),
            pltpu.VMEM((WIN, TILE, TILE), jnp.float32),
            pltpu.VMEM((WIN, TILE, 2 * TILE), qg.dtype),
            pltpu.SemaphoreType.DMA((4,)),
        ],
        compiler_params=pltpu.CompilerParams(vmem_limit_bytes=40 * 1024 * 1024),
        cost_estimate=pl.CostEstimate(
            flops=tiles * WIN * 10 * TILE * TILE * PAIR,
            bytes_accessed=rows * PAIR * 16,
            transcendentals=tiles * WIN * TILE * TILE,
        ),
        name="attend",
    )(slots, qg, own, prev, after)


def regroup(x):
    return lax.all_to_all(x, "heads", split_axis=0, concat_axis=0, tiled=True)


def to_neighbours(to_prev, to_next):
    count = lax.axis_size("frames")
    up = [(i, i + 1) for i in range(count - 1)]
    down = [(target, source) for source, target in up]
    from_prev = lax.ppermute(to_next, "frames", up)
    from_next = lax.ppermute(to_prev, "frames", down)
    return from_prev, from_next


def local(queries, keys, values, out_grad, windows):
    groups = lax.axis_size("heads")
    chunks = queries.shape[1] // (groups * HEAD_DIM)
    rows = queries.shape[0] * groups
    tiles = rows // TILE
    frame = lax.axis_index("frames")
    lists = lax.dynamic_slice_in_dim(windows, frame * tiles, tiles, 0)
    slots = jnp.where(lists >= 0, lists - (frame - 1) * tiles, -1)
    outs = ()
    for c in range(chunks):
        kv = regroup(pack(keys, values, c, groups)).reshape(rows, PAIR)
        qg = regroup(pack(queries, out_grad, c, groups)).reshape(rows, PAIR)
        prev, after = to_neighbours(kv, kv)
        dq, dprev, down, dnext = attend(slots, qg, kv, prev, after)
        from_prev, from_next = to_neighbours(dprev, dnext)
        dkv = (down + from_prev.astype(jnp.float32) + from_next.astype(jnp.float32)).astype(
            queries.dtype
        )
        dq = regroup(dq.reshape(groups, -1, HEAD_DIM))
        dkv = regroup(dkv.reshape(groups, -1, PAIR))
        outs = unpack(dq, dkv, outs, c, chunks)
    return tuple(outs)


def solution(mesh):
    spec = P(("frames", "heads"), None)
    return jax.shard_map(
        local, mesh=mesh, in_specs=(spec,) * 4 + (P(),), out_specs=(spec,) * 3, check_vma=False
    )
```

```python
import functools

import jax
import jax.numpy as jnp
from jax import lax
from jax.experimental import pallas as pl
from jax.experimental.pallas import tpu as pltpu
from jax.sharding import PartitionSpec as P

HEAD_DIM = 128
TILE = 384
WIN = 5
PAIR = 2 * HEAD_DIM
SPAN = WIN * TILE
SUB = 128
VMEM = 60 * 1024 * 1024
NEG = -1e30
LOG2E = 1.4426950408889634
NT = (((1,), (1,)), ((), ()))
TN = (((0,), (0,)), ((), ()))


def pack_kernel(groups, widths, *refs):
    ins, outs = refs[: sum(widths)], refs[sum(widths) :]
    first = 0
    for out_ref, width in zip(outs, widths):
        for i in range(width):
            for g in range(groups):
                out_ref[g, :, i * HEAD_DIM : (i + 1) * HEAD_DIM] = ins[first + i][
                    :, g * HEAD_DIM : (g + 1) * HEAD_DIM
                ]
        first += width


def pack(groups, messages):
    parts = [part for message in messages for part in message]
    rows = parts[0][0].shape[0]
    widths = [len(message) for message in messages]
    return pl.pallas_call(
        functools.partial(pack_kernel, groups, widths),
        grid=(1,),
        out_shape=[
            jax.ShapeDtypeStruct((groups, rows, width * HEAD_DIM), parts[0][0].dtype)
            for width in widths
        ],
        in_specs=[
            pl.BlockSpec((rows, groups * HEAD_DIM), lambda i, c=c: (0, c)) for _, c in parts
        ],
        out_specs=[
            pl.BlockSpec((groups, rows, width * HEAD_DIM), lambda i: (0, 0, 0))
            for width in widths
        ],
        cost_estimate=pl.CostEstimate(
            flops=0,
            bytes_accessed=len(parts) * groups * rows * HEAD_DIM * 4,
            transcendentals=0,
        ),
        compiler_params=pltpu.CompilerParams(vmem_limit_bytes=VMEM),
        name="pack",
    )(*[array for array, _ in parts])


def unpack_kernel(groups, plan, count, *refs):
    for source, lane, out, column in plan:
        for g in range(groups):
            start = column + g * HEAD_DIM
            refs[out][:, start : start + HEAD_DIM] = refs[source][
                g, :, lane : lane + HEAD_DIM
            ]


def attend_kernel(
    tiles,
    lanes_at,
    slot_ref,
    qg_hbm,
    own_hbm,
    prev_hbm,
    next_hbm,
    dq_hbm,
    dprev_hbm,
    down_hbm,
    dnext_hbm,
    dq_ref,
    dprev_ref,
    down_ref,
    dnext_ref,
    qg_ref,
    kv_ref,
    acc_ref,
    both_ref,
    score_ref,
    pgrad_ref,
    grad_ref,
    list_ref,
    sems,
):
    rows = tiles * TILE
    qg_lane, own_lane = lanes_at
    copies = [
        pltpu.make_async_copy(qg_hbm.at[:, pl.ds(qg_lane, PAIR)], qg_ref, sems.at[0]),
        pltpu.make_async_copy(
            own_hbm.at[:, pl.ds(own_lane, PAIR)], kv_ref.at[pl.ds(rows, rows)], sems.at[1]
        ),
        pltpu.make_async_copy(prev_hbm, kv_ref.at[pl.ds(0, rows)], sems.at[2]),
        pltpu.make_async_copy(next_hbm, kv_ref.at[pl.ds(2 * rows, rows)], sems.at[3]),
    ]
    for copy in copies:
        copy.start()
    acc_ref[...] = jnp.zeros_like(acc_ref)
    both_ref[...] = jnp.zeros_like(both_ref)
    for copy in copies:
        copy.wait()
    factor = HEAD_DIM ** (-0.5)
    scale = factor * LOG2E

    for t in range(tiles):
        here = slice(t * TILE, (t + 1) * TILE)
        query, grad = qg_ref[here, :HEAD_DIM], qg_ref[here, HEAD_DIM:]
        both_ref[:TILE, :HEAD_DIM] = query
        both_ref[TILE:, HEAD_DIM:] = grad
        used = [slot_ref[t, j] >= 0 for j in range(WIN)]
        places = [
            pl.multiple_of(jnp.maximum(slot_ref[t, j], 0) * TILE, TILE) for j in range(WIN)
        ]
        for j in range(WIN):
            list_ref[j * TILE : (j + 1) * TILE, :] = kv_ref[pl.ds(places[j], TILE), :]
        score_ref[...] = lax.dot_general(
            list_ref[:, :HEAD_DIM], query, NT, preferred_element_type=jnp.float32
        )
        pgrad_ref[...] = lax.dot_general(
            list_ref[:, HEAD_DIM:], grad, NT, preferred_element_type=jnp.float32
        )
        top = jnp.full((1, TILE), NEG, jnp.float32)
        for j in range(WIN):
            high = jnp.max(score_ref[j * TILE : (j + 1) * TILE, :], axis=0, keepdims=True)
            top = jnp.maximum(top, jnp.where(used[j], high, NEG))
        top = top * scale
        total = jnp.zeros((1, TILE), jnp.float32)
        for start in range(0, SPAN, SUB):
            part = slice(start, start + SUB)
            shift = jnp.where(used[start // TILE], top, -NEG)
            weight = jnp.exp2(score_ref[part, :] * scale - shift)
            score_ref[part, :] = weight
            total = total + jnp.sum(weight, axis=0, keepdims=True)
        inverse = 1.0 / total
        row_dot = jnp.zeros((1, TILE), jnp.float32)
        for start in range(0, SPAN, SUB):
            part = slice(start, start + SUB)
            prob = (score_ref[part, :] * inverse).astype(jnp.bfloat16)
            grad_ref[part, TILE:] = prob
            row_dot = row_dot + jnp.sum(
                prob.astype(jnp.float32) * pgrad_ref[part, :], axis=0, keepdims=True
            )
        for start in range(0, SPAN, SUB):
            part = slice(start, start + SUB)
            weight = score_ref[part, :] * inverse
            grad_ref[part, :TILE] = (weight * (pgrad_ref[part, :] - row_dot)).astype(
                jnp.bfloat16
            )
        terms = jnp.dot(grad_ref[...], both_ref[...], preferred_element_type=jnp.float32)
        for j in range(WIN):
            acc_ref[pl.ds(places[j], TILE), :] += terms[j * TILE : (j + 1) * TILE]
        dq = lax.dot_general(
            grad_ref[:, :TILE], list_ref[:, :HEAD_DIM], TN, preferred_element_type=jnp.float32
        )
        dq_ref[here, :] = (dq * factor).astype(dq_ref.dtype)

    lanes = lax.broadcasted_iota(jnp.int32, (1, PAIR), 1)
    side = jnp.where(lanes < HEAD_DIM, jnp.float32(factor), jnp.float32(1.0))
    back = [
        pltpu.make_async_copy(dprev_ref, dprev_hbm, sems.at[4]),
        pltpu.make_async_copy(dnext_ref, dnext_hbm, sems.at[5]),
        pltpu.make_async_copy(down_ref, down_hbm, sems.at[6]),
        pltpu.make_async_copy(dq_ref, dq_hbm, sems.at[7]),
    ]
    back[3].start()
    dprev_ref[...] = (acc_ref[:rows, :] * side).astype(dprev_ref.dtype)
    back[0].start()
    dnext_ref[...] = (acc_ref[2 * rows :, :] * side).astype(dnext_ref.dtype)
    back[1].start()
    down_ref[...] = acc_ref[rows : 2 * rows, :] * side
    back[2].start()
    for copy in back:
        copy.wait()


def attend(slots, qg, own, prev, after):
    (qg, qg_lane), (own, own_lane) = qg, own
    rows = qg.shape[0]
    tiles = rows // TILE
    hbm = pl.BlockSpec(memory_space=pl.ANY)
    return pl.pallas_call(
        functools.partial(attend_kernel, tiles, (qg_lane, own_lane)),
        out_shape=[
            jax.ShapeDtypeStruct((rows, HEAD_DIM), qg.dtype),
            jax.ShapeDtypeStruct((rows, PAIR), qg.dtype),
            jax.ShapeDtypeStruct((rows, PAIR), jnp.float32),
            jax.ShapeDtypeStruct((rows, PAIR), qg.dtype),
        ],
        in_specs=[pl.BlockSpec(memory_space=pltpu.SMEM)] + [hbm] * 4,
        out_specs=[hbm] * 4,
        scratch_shapes=[
            pltpu.VMEM((rows, HEAD_DIM), qg.dtype),
            pltpu.VMEM((rows, PAIR), qg.dtype),
            pltpu.VMEM((rows, PAIR), jnp.float32),
            pltpu.VMEM((rows, PAIR), qg.dtype),
            pltpu.VMEM((rows, PAIR), qg.dtype),
            pltpu.VMEM((3 * rows, PAIR), qg.dtype),
            pltpu.VMEM((3 * rows, PAIR), jnp.float32),
            pltpu.VMEM((2 * TILE, PAIR), qg.dtype),
            pltpu.VMEM((SPAN, TILE), jnp.float32),
            pltpu.VMEM((SPAN, TILE), jnp.float32),
            pltpu.VMEM((SPAN, 2 * TILE), qg.dtype),
            pltpu.VMEM((SPAN, PAIR), qg.dtype),
            pltpu.SemaphoreType.DMA((8,)),
        ],
        compiler_params=pltpu.CompilerParams(vmem_limit_bytes=VMEM),
        cost_estimate=pl.CostEstimate(
            flops=tiles * WIN * 14 * TILE * TILE * PAIR,
            bytes_accessed=rows * PAIR * 16,
            transcendentals=tiles * WIN * TILE * TILE,
        ),
        name="attend",
    )(slots, qg, own, prev, after)


def combine_kernel(queries, sums, blocks, *refs):
    ins, out_ref = refs[: queries + 3 * sums], refs[queries + 3 * sums]
    dq_ref, sum_ref, own_ref, low_ref, high_ref, sems = refs[queries + 3 * sums + 1 :]
    rows = out_ref.shape[0]
    size = rows // blocks
    copies = []
    loads = {}
    for i in range(queries):
        loads[i] = pltpu.make_async_copy(
            ins[i], dq_ref.at[:, pl.ds(i * HEAD_DIM, HEAD_DIM)], sems.at[blocks, i]
        )
        loads[i].start()
    for i in range(sums):
        for b in range(blocks):
            part = pl.ds(b * size, size)
            for k, ref in enumerate((own_ref, low_ref, high_ref)):
                loads[i, b, k] = pltpu.make_async_copy(
                    ins[queries + 3 * i + k].at[part, :], ref.at[i, part, :], sems.at[b, 4 * i + k]
                )
                loads[i, b, k].start()
    if queries:
        for i in range(queries):
            loads[i].wait()
        copy = pltpu.make_async_copy(
            dq_ref.at[:, pl.ds(0, queries * HEAD_DIM)],
            out_ref.at[:, pl.ds(0, queries * HEAD_DIM)],
            sems.at[blocks, queries],
        )
        copy.start()
        copies.append(copy)
    for i in range(sums):
        for b in range(blocks):
            part = pl.ds(b * size, size)
            for k in range(3):
                loads[i, b, k].wait()
            total = (
                own_ref[i, part, :]
                + low_ref[i, part, :].astype(jnp.float32)
                + high_ref[i, part, :].astype(jnp.float32)
            )
            sum_ref[i, part, :] = total.astype(sum_ref.dtype)
            copy = pltpu.make_async_copy(
                sum_ref.at[i, part, :],
                out_ref.at[part, pl.ds(queries * HEAD_DIM + i * PAIR, PAIR)],
                sems.at[b, 4 * i + 3],
            )
            copy.start()
            copies.append(copy)
    for copy in copies:
        copy.wait()


def combine(groups, queries, sums):
    parts = list(queries) + [part for terms in sums for part in terms]
    rows = parts[0].shape[0]
    count = len(sums)
    width = len(queries) * HEAD_DIM + count * PAIR
    blocks = 4
    hbm = pl.BlockSpec(memory_space=pl.ANY)
    out = pl.pallas_call(
        functools.partial(combine_kernel, len(queries), count, blocks),
        out_shape=jax.ShapeDtypeStruct((rows, width), jnp.bfloat16),
        in_specs=[hbm] * len(parts),
        out_specs=hbm,
        scratch_shapes=[
            pltpu.VMEM((rows, max(len(queries), 1) * HEAD_DIM), jnp.bfloat16),
            pltpu.VMEM((count, rows, PAIR), jnp.bfloat16),
            pltpu.VMEM((count, rows, PAIR), jnp.float32),
            pltpu.VMEM((count, rows, PAIR), jnp.bfloat16),
            pltpu.VMEM((count, rows, PAIR), jnp.bfloat16),
            pltpu.SemaphoreType.DMA((blocks + 1, 4 * max(count, 1))),
        ],
        cost_estimate=pl.CostEstimate(
            flops=0, bytes_accessed=rows * width * 6, transcendentals=0
        ),
        compiler_params=pltpu.CompilerParams(vmem_limit_bytes=VMEM),
        name="combine",
    )(*parts)
    return out.reshape(groups, rows // groups, width)


def regroup(x):
    return lax.all_to_all(x, "heads", split_axis=0, concat_axis=0, tiled=True)


def to_neighbours(to_prev, to_next):
    count = lax.axis_size("frames")
    up = [(i, (i + 1) % count) for i in range(count)]
    down = [(target, source) for source, target in up]
    from_prev = lax.ppermute(to_next, "frames", up)
    from_next = lax.ppermute(to_prev, "frames", down)
    return from_prev, from_next


def local(queries, keys, values, out_grad, windows):
    groups = lax.axis_size("heads")
    block = queries.shape[0]
    rows = block * groups
    tiles = rows // TILE
    frame = lax.axis_index("frames")
    lists = lax.dynamic_slice_in_dim(windows, frame * tiles, tiles, 0)
    slots = jnp.where(lists >= 0, lists - (frame - 1) * tiles, -1)
    pair = lambda c: [(keys, c), (values, c)]
    side = lambda c: [(queries, c), (out_grad, c)]
    (first,) = pack(groups, [pair(0)])
    second, third = pack(groups, [side(0) + pair(1), pair(2) + side(1) + side(2)])
    kv_0 = regroup(first).reshape(rows, -1)
    kv_0, second = lax.optimization_barrier((kv_0, second))
    halo_0 = to_neighbours(kv_0, kv_0)
    second = regroup(second).reshape(rows, -1)
    halo_0, second, third = lax.optimization_barrier((halo_0, second, third))
    third = regroup(third).reshape(rows, -1)
    kv_1, kv_2 = second[:, PAIR:], third[:, :PAIR]
    halo_1 = to_neighbours(kv_1, kv_1)
    halo_2 = to_neighbours(kv_2, kv_2)
    dq_0, dprev, down, dnext = attend(slots, (second, 0), (kv_0, 0), *halo_0)
    sum_0 = (down, *to_neighbours(dprev, dnext))
    slots, dq_0 = lax.optimization_barrier((slots, dq_0))
    dq_1, dprev, down, dnext = attend(slots, (third, PAIR), (second, PAIR), *halo_1)
    sum_1 = (down, *to_neighbours(dprev, dnext))
    fourth = regroup(combine(groups, [dq_0, dq_1], [sum_0]))
    slots, dq_1 = lax.optimization_barrier((slots, dq_1))
    dq_2, dprev, down, dnext = attend(slots, (third, 2 * PAIR), (third, 0), *halo_2)
    sum_2 = (down, *to_neighbours(dprev, dnext))
    fifth = regroup(combine(groups, [dq_2], [sum_1]))
    sixth = regroup(combine(groups, [], [sum_2]))

    width = groups * HEAD_DIM
    full = jax.ShapeDtypeStruct(queries.shape, queries.dtype)
    outs = pl.pallas_call(
        functools.partial(
            unpack_kernel,
            groups,
            [
                (0, 0, 2, 0),
                (0, HEAD_DIM, 2, width),
                (1, 0, 2, 2 * width),
                (0, PAIR, 3, 0),
                (0, PAIR + HEAD_DIM, 4, 0),
                (1, HEAD_DIM, 3, width),
                (1, PAIR, 4, width),
            ],
            2,
        ),
        grid=(1,),
        out_shape=[full] * 3,
        in_specs=[
            pl.BlockSpec(fourth.shape, lambda i: (0, 0, 0)),
            pl.BlockSpec(fifth.shape, lambda i: (0, 0, 0)),
        ],
        out_specs=[pl.BlockSpec((block, 3 * width), lambda i: (0, 0))]
        + [pl.BlockSpec((block, 2 * width), lambda i: (0, 0))] * 2,
        compiler_params=pltpu.CompilerParams(vmem_limit_bytes=VMEM),
        name="unpack",
    )(fourth, fifth)
    last = pl.BlockSpec((block, width), lambda i: (0, 2))
    rest = pl.pallas_call(
        functools.partial(unpack_kernel, groups, [(0, 0, 3, 0), (0, HEAD_DIM, 4, 0)], 3),
        grid=(1,),
        out_shape=[full] * 2,
        in_specs=[pl.BlockSpec(sixth.shape, lambda i: (0, 0, 0))]
        + [pl.BlockSpec(memory_space=pl.ANY)] * 2,
        out_specs=[last] * 2,
        input_output_aliases={1: 0, 2: 1},
        compiler_params=pltpu.CompilerParams(vmem_limit_bytes=VMEM),
        name="unpack_last",
    )(sixth, outs[1], outs[2])
    return outs[0], rest[0], rest[1]


def solution(mesh):
    spec = P(("frames", "heads"), None)
    return jax.shard_map(
        local, mesh=mesh, in_specs=(spec,) * 4 + (P(),), out_specs=(spec,) * 3, check_vma=False
    )
```

```python
import functools

import jax
import jax.numpy as jnp
from jax import lax
from jax.experimental import pallas as pl
from jax.experimental.pallas import tpu as pltpu
from jax.sharding import PartitionSpec as P

HEAD_DIM = 128
TILE = 384
WIN = 5
PAIR = 2 * HEAD_DIM
SPAN = WIN * TILE
SUB = 128
MIB = 1024 * 1024
NEG = -1e30
LOG2E = 1.4426950408889634
NT = (((1,), (1,)), ((), ()))
TN = (((0,), (0,)), ((), ()))


STEPS = ((0, 0), (2, 0), (2, 1), (1, 0), (3, 0), (1, 1), (3, 1), (0, 1))


def partner(me, step, groups):
    chips = groups // 2
    chip, core = me // 2, me % 2
    over, swap = step
    core = core + swap - 2 * core * swap
    return ((chip + over) % chips) * 2 + core, ((chip + chips - over) % chips) * 2 + core


def exchange(pieces, groups):
    out = [pieces[0]]
    for piece, step in zip(pieces[1:], STEPS[1:]):
        pairs = [(i, partner(i, step, groups)[0]) for i in range(groups)]
        out.append(lax.ppermute(piece, "heads", pairs))
    return out


def pack_kernel(groups, widths, *refs):
    ins, outs = refs[: sum(widths)], refs[sum(widths) :]
    first = 0
    for out_ref, width in zip(outs, widths):
        for i in range(width):
            for g in range(groups):
                out_ref[g, :, i * HEAD_DIM : (i + 1) * HEAD_DIM] = ins[first + i][
                    :, g * HEAD_DIM : (g + 1) * HEAD_DIM
                ]
        first += width


def pack(groups, messages):
    parts = [part for message in messages for part in message]
    rows = parts[0][0].shape[0]
    widths = [len(message) for message in messages]
    return pl.pallas_call(
        functools.partial(pack_kernel, groups, widths),
        grid=(1,),
        out_shape=[
            jax.ShapeDtypeStruct((groups, rows, width * HEAD_DIM), parts[0][0].dtype)
            for width in widths
        ],
        in_specs=[
            pl.BlockSpec((rows, groups * HEAD_DIM), lambda i, c=c: (0, c)) for _, c in parts
        ],
        out_specs=[
            pl.BlockSpec((groups, rows, width * HEAD_DIM), lambda i: (0, 0, 0))
            for width in widths
        ],
        cost_estimate=pl.CostEstimate(
            flops=0,
            bytes_accessed=len(parts) * groups * rows * HEAD_DIM * 4,
            transcendentals=0,
        ),
        compiler_params=pltpu.CompilerParams(vmem_limit_bytes=60 * MIB),
        name="pack",
    )(*[array for array, _ in parts])


def unpack_kernel(groups, plan, *refs):
    for source, lane, out, column in plan:
        for g in range(groups):
            start = column + g * HEAD_DIM
            refs[out][:, start : start + HEAD_DIM] = refs[source][
                g, :, lane : lane + HEAD_DIM
            ]


def unpack_pieces_kernel(groups, plan, outs_at, me_ref, *refs):
    for first, lane, out, column in plan:
        for s, step in enumerate(STEPS):
            _, source = partner(me_ref[0], step, groups)
            cols = pl.multiple_of(column + source * HEAD_DIM, HEAD_DIM)
            refs[outs_at + out][:, pl.ds(cols, HEAD_DIM)] = refs[first + s][
                :, lane : lane + HEAD_DIM
            ]


def attend_kernel(
    tiles,
    lanes_at,
    slot_ref,
    qg_hbm,
    own_hbm,
    prev_hbm,
    next_hbm,
    dq_hbm,
    dprev_hbm,
    down_hbm,
    dnext_hbm,
    dq_ref,
    dprev_ref,
    down_ref,
    dnext_ref,
    qg_ref,
    kv_ref,
    acc_ref,
    both_ref,
    score_ref,
    pgrad_ref,
    grad_ref,
    list_ref,
    key_ref,
    turned_ref,
    sems,
):
    rows = tiles * TILE
    qg_lane, own_lane = lanes_at
    copies = [
        pltpu.make_async_copy(qg_hbm.at[:, pl.ds(qg_lane, PAIR)], qg_ref, sems.at[0]),
        pltpu.make_async_copy(
            own_hbm.at[:, pl.ds(own_lane, PAIR)], kv_ref.at[pl.ds(rows, rows)], sems.at[1]
        ),
        pltpu.make_async_copy(prev_hbm, kv_ref.at[pl.ds(0, rows)], sems.at[2]),
        pltpu.make_async_copy(next_hbm, kv_ref.at[pl.ds(2 * rows, rows)], sems.at[3]),
    ]
    for copy in copies:
        copy.start()
    acc_ref[...] = jnp.zeros_like(acc_ref)
    both_ref[...] = jnp.zeros_like(both_ref)
    for copy, place in zip(copies, (None, 1, 0, 2)):
        copy.wait()
        for i in range(tiles) if place is not None else ():
            part = pl.ds(place * rows + i * TILE, TILE)
            key_ref[:, part] = kv_ref[part, :HEAD_DIM].T
    factor = HEAD_DIM ** (-0.5)
    scale = factor * LOG2E
    slots = [[slot_ref[t, j] for j in range(WIN)] for t in range(tiles)]
    places = [
        [pl.multiple_of(jnp.maximum(slot, 0) * TILE, TILE) for slot in row] for row in slots
    ]

    def scores(t):
        b = t % 2
        here = slice(t * TILE, (t + 1) * TILE)
        query, grad = qg_ref[here, :HEAD_DIM], qg_ref[here, HEAD_DIM:]
        both_ref[b, :TILE, :HEAD_DIM] = query
        both_ref[b, TILE:, HEAD_DIM:] = grad
        for j in range(WIN):
            list_ref[b, j * TILE : (j + 1) * TILE, :] = kv_ref[pl.ds(places[t][j], TILE), :]
        score_ref[b] = lax.dot_general(
            list_ref[b, :, :HEAD_DIM], query, NT, preferred_element_type=jnp.float32
        )
        pgrad_ref[b] = lax.dot_general(
            list_ref[b, :, HEAD_DIM:], grad, NT, preferred_element_type=jnp.float32
        )

    def weights(t):
        b = t % 2
        used = [slot >= 0 for slot in slots[t]]
        top = jnp.full((1, TILE), NEG, jnp.float32)
        for j in range(WIN):
            high = jnp.max(score_ref[b, j * TILE : (j + 1) * TILE, :], axis=0, keepdims=True)
            top = jnp.maximum(top, jnp.where(used[j], high, NEG))
        top = top * scale
        total = jnp.zeros((1, TILE), jnp.float32)
        for start in range(0, SPAN, SUB):
            part = slice(start, start + SUB)
            shift = jnp.where(used[start // TILE], top, -NEG)
            weight = jnp.exp2(score_ref[b, part, :] * scale - shift)
            score_ref[b, part, :] = weight
            total = total + jnp.sum(weight, axis=0, keepdims=True)
        inverse = 1.0 / total
        row_dot = jnp.zeros((1, TILE), jnp.float32)
        for start in range(0, SPAN, SUB):
            part = slice(start, start + SUB)
            prob = (score_ref[b, part, :] * inverse).astype(jnp.bfloat16)
            grad_ref[b, part, TILE:] = prob
            row_dot = row_dot + jnp.sum(
                prob.astype(jnp.float32) * pgrad_ref[b, part, :], axis=0, keepdims=True
            )
        for start in range(0, SPAN, SUB):
            part = slice(start, start + SUB)
            weight = score_ref[b, part, :] * inverse
            grad_ref[b, part, :TILE] = (
                weight * (pgrad_ref[b, part, :] - row_dot)
            ).astype(jnp.bfloat16)

    def key_terms(t):
        b = t % 2
        terms = jnp.dot(grad_ref[b], both_ref[b], preferred_element_type=jnp.float32)
        for j in range(WIN):
            acc_ref[pl.ds(places[t][j], TILE), :] += terms[j * TILE : (j + 1) * TILE]

    def query_terms(t):
        b = t % 2
        for j in range(WIN):
            turned_ref[b, :, j * TILE : (j + 1) * TILE] = key_ref[:, pl.ds(places[t][j], TILE)]
        dq = jnp.dot(turned_ref[b], grad_ref[b, :, :TILE], preferred_element_type=jnp.float32)
        dq_ref[t * TILE : (t + 1) * TILE, :] = (dq * factor).T.astype(dq_ref.dtype)

    scores(0)
    for t in range(tiles):
        if t == 0:
            scores(1)
        weights(t)
        if t > 0:
            query_terms(t - 1)
        if t > 0 and t + 1 < tiles:
            scores(t + 1)
        key_terms(t)
    query_terms(tiles - 1)

    lanes = lax.broadcasted_iota(jnp.int32, (1, PAIR), 1)
    side = jnp.where(lanes < HEAD_DIM, jnp.float32(factor), jnp.float32(1.0))
    back = [
        pltpu.make_async_copy(dprev_ref, dprev_hbm, sems.at[4]),
        pltpu.make_async_copy(dnext_ref, dnext_hbm, sems.at[5]),
        pltpu.make_async_copy(down_ref, down_hbm, sems.at[6]),
        pltpu.make_async_copy(dq_ref, dq_hbm, sems.at[7]),
    ]
    back[3].start()
    dprev_ref[...] = (acc_ref[:rows, :] * side).astype(dprev_ref.dtype)
    back[0].start()
    dnext_ref[...] = (acc_ref[2 * rows :, :] * side).astype(dnext_ref.dtype)
    back[1].start()
    down_ref[...] = acc_ref[rows : 2 * rows, :] * side
    back[2].start()
    for copy in back:
        copy.wait()


def attend(slots, qg, own, prev, after):
    (qg, qg_lane), (own, own_lane) = qg, own
    rows = qg.shape[0]
    tiles = rows // TILE
    hbm = pl.BlockSpec(memory_space=pl.ANY)
    return pl.pallas_call(
        functools.partial(attend_kernel, tiles, (qg_lane, own_lane)),
        out_shape=[
            jax.ShapeDtypeStruct((rows, HEAD_DIM), qg.dtype),
            jax.ShapeDtypeStruct((rows, PAIR), qg.dtype),
            jax.ShapeDtypeStruct((rows, PAIR), jnp.float32),
            jax.ShapeDtypeStruct((rows, PAIR), qg.dtype),
        ],
        in_specs=[pl.BlockSpec(memory_space=pltpu.SMEM)] + [hbm] * 4,
        out_specs=[hbm] * 4,
        scratch_shapes=[
            pltpu.VMEM((rows, HEAD_DIM), qg.dtype),
            pltpu.VMEM((rows, PAIR), qg.dtype),
            pltpu.VMEM((rows, PAIR), jnp.float32),
            pltpu.VMEM((rows, PAIR), qg.dtype),
            pltpu.VMEM((rows, PAIR), qg.dtype),
            pltpu.VMEM((3 * rows, PAIR), qg.dtype),
            pltpu.VMEM((3 * rows, PAIR), jnp.float32),
            pltpu.VMEM((2, 2 * TILE, PAIR), qg.dtype),
            pltpu.VMEM((2, SPAN, TILE), jnp.float32),
            pltpu.VMEM((2, SPAN, TILE), jnp.float32),
            pltpu.VMEM((2, SPAN, 2 * TILE), qg.dtype),
            pltpu.VMEM((2, SPAN, PAIR), qg.dtype),
            pltpu.VMEM((HEAD_DIM, 3 * rows), qg.dtype),
            pltpu.VMEM((2, HEAD_DIM, SPAN), qg.dtype),
            pltpu.SemaphoreType.DMA((8,)),
        ],
        compiler_params=pltpu.CompilerParams(vmem_limit_bytes=38 * MIB),
        cost_estimate=pl.CostEstimate(
            flops=tiles * WIN * 14 * TILE * TILE * PAIR,
            bytes_accessed=rows * PAIR * 16,
            transcendentals=tiles * WIN * TILE * TILE,
        ),
        name="attend",
    )(slots, qg, own, prev, after)


def combine_kernel(queries, sums, groups, apart, me_ref, *refs):
    count = queries + 3 * sums
    ins, outs = refs[:count], refs[count : -5]
    all_ref, own_ref, low_ref, high_ref, sems = refs[-5:]
    rows = all_ref.shape[0]
    blocks = 4
    size = rows // blocks
    lead = queries * HEAD_DIM
    loads = []
    for i in range(queries):
        lanes = pl.ds(i * HEAD_DIM, HEAD_DIM)
        loads.append(pltpu.make_async_copy(ins[i], all_ref.at[:, lanes], sems.at[blocks, i]))
    terms = {}
    for i in range(sums):
        for b in range(blocks):
            part = pl.ds(b * size, size)
            for k, ref in enumerate((own_ref, low_ref, high_ref)):
                terms[i, b, k] = pltpu.make_async_copy(
                    ins[queries + 3 * i + k].at[part, :], ref.at[i, part, :], sems.at[b, 3 * i + k]
                )
                terms[i, b, k].start()
    for copy in loads:
        copy.start()
    for i in range(sums):
        for b in range(blocks):
            part = pl.ds(b * size, size)
            for k in range(3):
                terms[i, b, k].wait()
            total = (
                own_ref[i, part, :]
                + low_ref[i, part, :].astype(jnp.float32)
                + high_ref[i, part, :].astype(jnp.float32)
            )
            all_ref[part, lead + i * PAIR : lead + (i + 1) * PAIR] = total.astype(all_ref.dtype)
    for copy in loads:
        copy.wait()
    backs = []
    if apart:
        block = rows // groups
        for s, step in enumerate(STEPS):
            target, _ = partner(me_ref[0], step, groups)
            part = pl.ds(pl.multiple_of(target * block, block), block)
            backs.append(
                pltpu.make_async_copy(all_ref.at[part, :], outs[s], sems.at[blocks + 1 + s, 0])
            )
    else:
        backs.append(pltpu.make_async_copy(all_ref, outs[0], sems.at[blocks + 1, 0]))
    for copy in backs:
        copy.start()
    for copy in backs:
        copy.wait()


def combine(me, groups, queries, sums, apart):
    parts = list(queries) + [part for terms in sums for part in terms]
    rows = parts[0].shape[0]
    count = len(sums)
    width = len(queries) * HEAD_DIM + count * PAIR
    hbm = pl.BlockSpec(memory_space=pl.ANY)
    shape = (rows // groups, width) if apart else (rows, width)
    outs = pl.pallas_call(
        functools.partial(combine_kernel, len(queries), count, groups, apart),
        out_shape=[jax.ShapeDtypeStruct(shape, jnp.bfloat16)] * (groups if apart else 1),
        in_specs=[pl.BlockSpec(memory_space=pltpu.SMEM)] + [hbm] * len(parts),
        out_specs=[hbm] * (groups if apart else 1),
        scratch_shapes=[
            pltpu.VMEM((rows, width), jnp.bfloat16),
            pltpu.VMEM((count, rows, PAIR), jnp.float32),
            pltpu.VMEM((count, rows, PAIR), jnp.bfloat16),
            pltpu.VMEM((count, rows, PAIR), jnp.bfloat16),
            pltpu.SemaphoreType.DMA((5 + groups, 3 * count)),
        ],
        compiler_params=pltpu.CompilerParams(vmem_limit_bytes=12 * MIB),
        cost_estimate=pl.CostEstimate(
            flops=0, bytes_accessed=rows * width * 6, transcendentals=0
        ),
        name="combine",
    )(me, *parts)
    return outs if apart else outs[0].reshape(groups, rows // groups, width)


def regroup(x):
    return lax.all_to_all(x, "heads", split_axis=0, concat_axis=0, tiled=True)


def to_neighbours(to_prev, to_next):
    count = lax.axis_size("frames")
    up = [(i, (i + 1) % count) for i in range(count)]
    down = [(target, source) for source, target in up]
    from_prev = lax.ppermute(to_next, "frames", up)
    from_next = lax.ppermute(to_prev, "frames", down)
    return from_prev, from_next


def local(queries, keys, values, out_grad, windows):
    groups = lax.axis_size("heads")
    block = queries.shape[0]
    rows = block * groups
    tiles = rows // TILE
    frame = lax.axis_index("frames")
    lists = lax.dynamic_slice_in_dim(windows, frame * tiles, tiles, 0)
    slots = jnp.where(lists >= 0, lists - (frame - 1) * tiles, -1)
    me = lax.axis_index("heads").astype(jnp.int32).reshape(1)
    pair = lambda c: [(keys, c), (values, c)]
    side = lambda c: [(queries, c), (out_grad, c)]
    (first,) = pack(groups, [pair(0)])
    second, third = pack(groups, [side(0) + pair(1), pair(2) + side(1) + side(2)])
    kv_0 = regroup(first).reshape(rows, -1)
    kv_0, second = lax.optimization_barrier((kv_0, second))
    halo_0 = to_neighbours(kv_0, kv_0)
    second = regroup(second).reshape(rows, -1)
    halo_0, second, third = lax.optimization_barrier((halo_0, second, third))
    third = regroup(third).reshape(rows, -1)
    kv_1, kv_2 = second[:, PAIR:], third[:, :PAIR]
    halo_1 = to_neighbours(kv_1, kv_1)
    halo_2 = to_neighbours(kv_2, kv_2)
    dq_0, dprev, down, dnext = attend(slots, (second, 0), (kv_0, 0), *halo_0)
    sum_0 = (down, *to_neighbours(dprev, dnext))
    slots, dq_0 = lax.optimization_barrier((slots, dq_0))
    dq_1, dprev, down, dnext = attend(slots, (third, PAIR), (second, PAIR), *halo_1)
    sum_1 = (down, *to_neighbours(dprev, dnext))
    fourth = regroup(combine(me, groups, [dq_0, dq_1], [sum_0], False))
    slots, dq_1 = lax.optimization_barrier((slots, dq_1))
    dq_2, dprev, down, dnext = attend(slots, (third, 2 * PAIR), (third, 0), *halo_2)
    sum_2 = (down, *to_neighbours(dprev, dnext))
    width = groups * HEAD_DIM
    full = jax.ShapeDtypeStruct(queries.shape, queries.dtype)
    params = pltpu.CompilerParams(vmem_limit_bytes=24 * MIB)
    column = lambda start, wide: pl.BlockSpec((block, wide * width), lambda i: (0, start))
    outs = pl.pallas_call(
        functools.partial(
            unpack_kernel,
            groups,
            [
                (0, 0, 1, 0),
                (0, HEAD_DIM, 1, width),
                (0, PAIR, 2, 0),
                (0, PAIR + HEAD_DIM, 3, 0),
            ],
        ),
        grid=(1,),
        out_shape=[full] * 3,
        in_specs=[pl.BlockSpec(fourth.shape, lambda i: (0, 0, 0))],
        out_specs=[column(0, 2), column(0, 1), column(0, 1)],
        compiler_params=params,
        name="unpack",
    )(fourth)
    outs, sum_1 = lax.optimization_barrier((tuple(outs), sum_1))
    fifth = exchange(combine(me, groups, [dq_2], [sum_1], True), groups)
    sixth = exchange(combine(me, groups, [], [sum_2], True), groups)
    steps = len(STEPS)
    tail = pl.BlockSpec((pl.Element(block), pl.Element(2 * width)), lambda i: (0, width))
    steps = len(STEPS)
    whole = lambda piece: pl.BlockSpec(piece.shape, lambda i: (0, 0))
    return tuple(
        pl.pallas_call(
            functools.partial(
                unpack_pieces_kernel,
                groups,
                [
                    (0, 0, 0, 0),
                    (0, HEAD_DIM, 1, 0),
                    (0, PAIR, 2, 0),
                    (steps, 0, 1, width),
                    (steps, HEAD_DIM, 2, width),
                ],
                2 * steps + 3,
            ),
            grid=(1,),
            out_shape=[full] * 3,
            in_specs=[pl.BlockSpec(memory_space=pltpu.SMEM)]
            + [whole(piece) for piece in (*fifth, *sixth)]
            + [pl.BlockSpec(memory_space=pl.ANY)] * 3,
            out_specs=[column(2, 1), tail, tail],
            input_output_aliases={1 + 2 * steps + i: i for i in range(3)},
            compiler_params=params,
            name="unpack_last",
        )(me, *fifth, *sixth, *outs)
    )


def solution(mesh):
    spec = P(("frames", "heads"), None)
    return jax.shard_map(
        local, mesh=mesh, in_specs=(spec,) * 4 + (P(),), out_specs=(spec,) * 3, check_vma=False
    )
```

```python
import functools

import jax
import jax.numpy as jnp
from jax import lax
from jax.experimental import pallas as pl
from jax.experimental.pallas import tpu as pltpu
from jax.sharding import PartitionSpec as P

HEAD_DIM = 128
TILE = 384
WIN = 5
PAIR = 2 * HEAD_DIM
SPAN = WIN * TILE
SUB = 128
MIB = 1024 * 1024
NEG = -1e30
LOG2E = 1.4426950408889634
NT = (((1,), (1,)), ((), ()))
TN = (((0,), (0,)), ((), ()))


STEPS = ((0, 0), (2, 0), (2, 1), (1, 0), (3, 0), (1, 1), (3, 1), (0, 1))


def partner(me, step, groups):
    chips = groups // 2
    chip, core = me // 2, me % 2
    over, swap = step
    core = core + swap - 2 * core * swap
    return ((chip + over) % chips) * 2 + core, ((chip + chips - over) % chips) * 2 + core


def exchange(pieces, groups):
    out = [pieces[0]]
    for piece, step in zip(pieces[1:], STEPS[1:]):
        pairs = [(i, partner(i, step, groups)[0]) for i in range(groups)]
        out.append(lax.ppermute(piece, "heads", pairs))
    return out


def pack_kernel(groups, widths, *refs):
    ins, outs = refs[: sum(widths)], refs[sum(widths) :]
    first = 0
    for out_ref, width in zip(outs, widths):
        for i in range(width):
            for g in range(groups):
                out_ref[g, :, i * HEAD_DIM : (i + 1) * HEAD_DIM] = ins[first + i][
                    :, g * HEAD_DIM : (g + 1) * HEAD_DIM
                ]
        first += width


def pack(groups, messages):
    parts = [part for message in messages for part in message]
    rows = parts[0][0].shape[0]
    widths = [len(message) for message in messages]
    return pl.pallas_call(
        functools.partial(pack_kernel, groups, widths),
        grid=(1,),
        out_shape=[
            jax.ShapeDtypeStruct((groups, rows, width * HEAD_DIM), parts[0][0].dtype)
            for width in widths
        ],
        in_specs=[
            pl.BlockSpec((rows, groups * HEAD_DIM), lambda i, c=c: (0, c)) for _, c in parts
        ],
        out_specs=[
            pl.BlockSpec((groups, rows, width * HEAD_DIM), lambda i: (0, 0, 0))
            for width in widths
        ],
        cost_estimate=pl.CostEstimate(
            flops=0,
            bytes_accessed=len(parts) * groups * rows * HEAD_DIM * 4,
            transcendentals=0,
        ),
        compiler_params=pltpu.CompilerParams(vmem_limit_bytes=60 * MIB),
        name="pack",
    )(*[array for array, _ in parts])


def unpack_kernel(groups, plan, *refs):
    for source, lane, out, column in plan:
        for g in range(groups):
            start = column + g * HEAD_DIM
            refs[out][:, start : start + HEAD_DIM] = refs[source][
                g, :, lane : lane + HEAD_DIM
            ]


def unpack_pieces_kernel(groups, plan, outs_at, me_ref, *refs):
    for first, lane, out, column in plan:
        for s, step in enumerate(STEPS):
            _, source = partner(me_ref[0], step, groups)
            cols = pl.multiple_of(column + source * HEAD_DIM, HEAD_DIM)
            refs[outs_at + out][:, pl.ds(cols, HEAD_DIM)] = refs[first + s][
                :, lane : lane + HEAD_DIM
            ]


def attend_kernel(
    tiles,
    lanes_at,
    slot_ref,
    qg_hbm,
    own_hbm,
    prev_hbm,
    next_hbm,
    dq_hbm,
    dprev_hbm,
    down_hbm,
    dnext_hbm,
    dq_ref,
    dprev_ref,
    down_ref,
    dnext_ref,
    qg_ref,
    kv_ref,
    acc_ref,
    both_ref,
    score_ref,
    pgrad_ref,
    grad_ref,
    list_ref,
    key_ref,
    turned_ref,
    sems,
):
    rows = tiles * TILE
    qg_lane, own_lane = lanes_at
    copies = [
        pltpu.make_async_copy(qg_hbm.at[:, pl.ds(qg_lane, PAIR)], qg_ref, sems.at[0]),
        pltpu.make_async_copy(
            own_hbm.at[:, pl.ds(own_lane, PAIR)], kv_ref.at[pl.ds(rows, rows)], sems.at[1]
        ),
        pltpu.make_async_copy(prev_hbm, kv_ref.at[pl.ds(0, rows)], sems.at[2]),
        pltpu.make_async_copy(next_hbm, kv_ref.at[pl.ds(2 * rows, rows)], sems.at[3]),
    ]
    for copy in copies:
        copy.start()
    acc_ref[...] = jnp.zeros_like(acc_ref)
    both_ref[...] = jnp.zeros_like(both_ref)
    for copy, place in zip(copies, (None, 1, 0, 2)):
        copy.wait()
        for i in range(tiles) if place is not None else ():
            part = pl.ds(place * rows + i * TILE, TILE)
            key_ref[:, part] = kv_ref[part, :HEAD_DIM].T
    factor = HEAD_DIM ** (-0.5)
    scale = factor * LOG2E
    slots = [[slot_ref[t, j] for j in range(WIN)] for t in range(tiles)]
    places = [
        [pl.multiple_of(jnp.maximum(slot, 0) * TILE, TILE) for slot in row] for row in slots
    ]

    def scores(t):
        b = t % 2
        here = slice(t * TILE, (t + 1) * TILE)
        query, grad = qg_ref[here, :HEAD_DIM], qg_ref[here, HEAD_DIM:]
        both_ref[b, :TILE, :HEAD_DIM] = query
        both_ref[b, TILE:, HEAD_DIM:] = grad
        for j in range(WIN):
            list_ref[b, j * TILE : (j + 1) * TILE, :] = kv_ref[pl.ds(places[t][j], TILE), :]
        score_ref[b] = lax.dot_general(
            list_ref[b, :, :HEAD_DIM], query, NT, preferred_element_type=jnp.float32
        )
        pgrad_ref[b] = lax.dot_general(
            list_ref[b, :, HEAD_DIM:], grad, NT, preferred_element_type=jnp.float32
        )

    def weights(t):
        b = t % 2
        used = [slot >= 0 for slot in slots[t]]
        top = jnp.full((1, TILE), NEG, jnp.float32)
        for j in range(WIN):
            high = jnp.max(score_ref[b, j * TILE : (j + 1) * TILE, :], axis=0, keepdims=True)
            top = jnp.maximum(top, jnp.where(used[j], high, NEG))
        top = top * scale
        total = jnp.zeros((1, TILE), jnp.float32)
        for start in range(0, SPAN, SUB):
            part = slice(start, start + SUB)
            shift = jnp.where(used[start // TILE], top, -NEG)
            weight = jnp.exp2(score_ref[b, part, :] * scale - shift)
            score_ref[b, part, :] = weight
            total = total + jnp.sum(weight, axis=0, keepdims=True)
        inverse = 1.0 / total
        row_dot = jnp.zeros((1, TILE), jnp.float32)
        for start in range(0, SPAN, SUB):
            part = slice(start, start + SUB)
            prob = (score_ref[b, part, :] * inverse).astype(jnp.bfloat16)
            grad_ref[b, part, TILE:] = prob
            row_dot = row_dot + jnp.sum(
                prob.astype(jnp.float32) * pgrad_ref[b, part, :], axis=0, keepdims=True
            )
        for start in range(0, SPAN, SUB):
            part = slice(start, start + SUB)
            weight = score_ref[b, part, :] * inverse
            grad_ref[b, part, :TILE] = (
                weight * (pgrad_ref[b, part, :] - row_dot)
            ).astype(jnp.bfloat16)

    def key_terms(t):
        b = t % 2
        terms = jnp.dot(grad_ref[b], both_ref[b], preferred_element_type=jnp.float32)
        for j in range(WIN):
            acc_ref[pl.ds(places[t][j], TILE), :] += terms[j * TILE : (j + 1) * TILE]

    def query_terms(t):
        b = t % 2
        for j in range(WIN):
            turned_ref[b, :, j * TILE : (j + 1) * TILE] = key_ref[:, pl.ds(places[t][j], TILE)]
        dq = jnp.dot(turned_ref[b], grad_ref[b, :, :TILE], preferred_element_type=jnp.float32)
        dq_ref[t * TILE : (t + 1) * TILE, :] = (dq * factor).T.astype(dq_ref.dtype)

    scores(0)
    for t in range(tiles):
        if t == 0:
            scores(1)
        weights(t)
        if t > 0:
            query_terms(t - 1)
        if t > 0 and t + 1 < tiles:
            scores(t + 1)
        key_terms(t)
    query_terms(tiles - 1)

    lanes = lax.broadcasted_iota(jnp.int32, (1, PAIR), 1)
    side = jnp.where(lanes < HEAD_DIM, jnp.float32(factor), jnp.float32(1.0))
    back = [
        pltpu.make_async_copy(dprev_ref, dprev_hbm, sems.at[4]),
        pltpu.make_async_copy(dnext_ref, dnext_hbm, sems.at[5]),
        pltpu.make_async_copy(down_ref, down_hbm, sems.at[6]),
        pltpu.make_async_copy(dq_ref, dq_hbm, sems.at[7]),
    ]
    back[3].start()
    dprev_ref[...] = (acc_ref[:rows, :] * side).astype(dprev_ref.dtype)
    back[0].start()
    dnext_ref[...] = (acc_ref[2 * rows :, :] * side).astype(dnext_ref.dtype)
    back[1].start()
    down_ref[...] = acc_ref[rows : 2 * rows, :] * side
    back[2].start()
    for copy in back:
        copy.wait()


def attend(slots, qg, own, prev, after, grant):
    (qg, qg_lane), (own, own_lane) = qg, own
    rows = qg.shape[0]
    tiles = rows // TILE
    hbm = pl.BlockSpec(memory_space=pl.ANY)
    return pl.pallas_call(
        functools.partial(attend_kernel, tiles, (qg_lane, own_lane)),
        out_shape=[
            jax.ShapeDtypeStruct((rows, HEAD_DIM), qg.dtype),
            jax.ShapeDtypeStruct((rows, PAIR), qg.dtype),
            jax.ShapeDtypeStruct((rows, PAIR), jnp.float32),
            jax.ShapeDtypeStruct((rows, PAIR), qg.dtype),
        ],
        in_specs=[pl.BlockSpec(memory_space=pltpu.SMEM)] + [hbm] * 4,
        out_specs=[hbm] * 4,
        scratch_shapes=[
            pltpu.VMEM((rows, HEAD_DIM), qg.dtype),
            pltpu.VMEM((rows, PAIR), qg.dtype),
            pltpu.VMEM((rows, PAIR), jnp.float32),
            pltpu.VMEM((rows, PAIR), qg.dtype),
            pltpu.VMEM((rows, PAIR), qg.dtype),
            pltpu.VMEM((3 * rows, PAIR), qg.dtype),
            pltpu.VMEM((3 * rows, PAIR), jnp.float32),
            pltpu.VMEM((2, 2 * TILE, PAIR), qg.dtype),
            pltpu.VMEM((2, SPAN, TILE), jnp.float32),
            pltpu.VMEM((2, SPAN, TILE), jnp.float32),
            pltpu.VMEM((2, SPAN, 2 * TILE), qg.dtype),
            pltpu.VMEM((2, SPAN, PAIR), qg.dtype),
            pltpu.VMEM((HEAD_DIM, 3 * rows), qg.dtype),
            pltpu.VMEM((2, HEAD_DIM, SPAN), qg.dtype),
            pltpu.SemaphoreType.DMA((8,)),
        ],
        compiler_params=pltpu.CompilerParams(vmem_limit_bytes=grant * MIB),
        cost_estimate=pl.CostEstimate(
            flops=tiles * WIN * 14 * TILE * TILE * PAIR,
            bytes_accessed=rows * PAIR * 16,
            transcendentals=tiles * WIN * TILE * TILE,
        ),
        name="attend",
    )(slots, qg, own, prev, after)


def combine_kernel(queries, sums, groups, apart, me_ref, *refs):
    count = queries + 3 * sums
    ins, outs = refs[:count], refs[count : -5]
    all_ref, own_ref, low_ref, high_ref, sems = refs[-5:]
    rows = all_ref.shape[0]
    blocks = 2
    size = rows // blocks
    lead = queries * HEAD_DIM
    loads = []
    for i in range(queries):
        lanes = pl.ds(i * HEAD_DIM, HEAD_DIM)
        loads.append(pltpu.make_async_copy(ins[i], all_ref.at[:, lanes], sems.at[blocks, i]))
    terms = {}
    for i in range(sums):
        for b in range(blocks):
            part = pl.ds(b * size, size)
            for k, ref in enumerate((own_ref, low_ref, high_ref)):
                terms[i, b, k] = pltpu.make_async_copy(
                    ins[queries + 3 * i + k].at[part, :], ref.at[i, part, :], sems.at[b, 3 * i + k]
                )
                terms[i, b, k].start()
    for copy in loads:
        copy.start()
    for i in range(sums):
        for b in range(blocks):
            part = pl.ds(b * size, size)
            for k in range(3):
                terms[i, b, k].wait()
            total = (
                own_ref[i, part, :]
                + low_ref[i, part, :].astype(jnp.float32)
                + high_ref[i, part, :].astype(jnp.float32)
            )
            all_ref[part, lead + i * PAIR : lead + (i + 1) * PAIR] = total.astype(all_ref.dtype)
    for copy in loads:
        copy.wait()
    backs = []
    if apart:
        block = rows // groups
        for s, step in enumerate(STEPS):
            target, _ = partner(me_ref[0], step, groups)
            part = pl.ds(pl.multiple_of(target * block, block), block)
            backs.append(
                pltpu.make_async_copy(all_ref.at[part, :], outs[s], sems.at[blocks + 1 + s, 0])
            )
    else:
        backs.append(pltpu.make_async_copy(all_ref, outs[0], sems.at[blocks + 1, 0]))
    for copy in backs:
        copy.start()
    for copy in backs:
        copy.wait()


def combine(me, groups, queries, sums, apart):
    parts = list(queries) + [part for terms in sums for part in terms]
    rows = parts[0].shape[0]
    count = len(sums)
    width = len(queries) * HEAD_DIM + count * PAIR
    hbm = pl.BlockSpec(memory_space=pl.ANY)
    shape = (rows // groups, width) if apart else (rows, width)
    outs = pl.pallas_call(
        functools.partial(combine_kernel, len(queries), count, groups, apart),
        out_shape=[jax.ShapeDtypeStruct(shape, jnp.bfloat16)] * (groups if apart else 1),
        in_specs=[pl.BlockSpec(memory_space=pltpu.SMEM)] + [hbm] * len(parts),
        out_specs=[hbm] * (groups if apart else 1),
        scratch_shapes=[
            pltpu.VMEM((rows, width), jnp.bfloat16),
            pltpu.VMEM((count, rows, PAIR), jnp.float32),
            pltpu.VMEM((count, rows, PAIR), jnp.bfloat16),
            pltpu.VMEM((count, rows, PAIR), jnp.bfloat16),
            pltpu.SemaphoreType.DMA((3 + groups, 3 * count)),
        ],
        compiler_params=pltpu.CompilerParams(vmem_limit_bytes=12 * MIB),
        cost_estimate=pl.CostEstimate(
            flops=0, bytes_accessed=rows * width * 6, transcendentals=0
        ),
        name="combine",
    )(me, *parts)
    return outs if apart else outs[0].reshape(groups, rows // groups, width)


def regroup(x):
    return lax.all_to_all(x, "heads", split_axis=0, concat_axis=0, tiled=True)


def to_neighbours(to_prev, to_next):
    count = lax.axis_size("frames")
    up = [(i, (i + 1) % count) for i in range(count)]
    down = [(target, source) for source, target in up]
    from_prev = lax.ppermute(to_next, "frames", up)
    from_next = lax.ppermute(to_prev, "frames", down)
    return from_prev, from_next


def local(queries, keys, values, out_grad, windows):
    groups = lax.axis_size("heads")
    block = queries.shape[0]
    rows = block * groups
    tiles = rows // TILE
    frame = lax.axis_index("frames")
    lists = lax.dynamic_slice_in_dim(windows, frame * tiles, tiles, 0)
    slots = jnp.where(lists >= 0, lists - (frame - 1) * tiles, -1)
    me = lax.axis_index("heads").astype(jnp.int32).reshape(1)
    pair = lambda c: [(keys, c), (values, c)]
    side = lambda c: [(queries, c), (out_grad, c)]
    (first,) = pack(groups, [pair(0)])
    second, third = pack(groups, [side(0) + pair(1), pair(2) + side(1) + side(2)])
    kv_0 = regroup(first).reshape(rows, -1)
    kv_0, second = lax.optimization_barrier((kv_0, second))
    halo_0 = to_neighbours(kv_0, kv_0)
    second = regroup(second).reshape(rows, -1)
    halo_0, second, third = lax.optimization_barrier((halo_0, second, third))
    third = regroup(third).reshape(rows, -1)
    kv_1, kv_2 = second[:, PAIR:], third[:, :PAIR]
    halo_1 = to_neighbours(kv_1, kv_1)
    halo_2 = to_neighbours(kv_2, kv_2)
    dq_0, dprev, down, dnext = attend(slots, (second, 0), (kv_0, 0), *halo_0, 60)
    sum_0 = (down, *to_neighbours(dprev, dnext))
    slots, dq_0 = lax.optimization_barrier((slots, dq_0))
    dq_1, dprev, down, dnext = attend(slots, (third, PAIR), (second, PAIR), *halo_1, 38)
    sum_1 = (down, *to_neighbours(dprev, dnext))
    fourth = regroup(combine(me, groups, [dq_0, dq_1], [sum_0], False))
    slots, dq_1 = lax.optimization_barrier((slots, dq_1))
    dq_2, dprev, down, dnext = attend(slots, (third, 2 * PAIR), (third, 0), *halo_2, 60)
    sum_2 = (down, *to_neighbours(dprev, dnext))
    width = groups * HEAD_DIM
    full = jax.ShapeDtypeStruct(queries.shape, queries.dtype)
    params = pltpu.CompilerParams(vmem_limit_bytes=24 * MIB)
    column = lambda start, wide: pl.BlockSpec((block, wide * width), lambda i: (0, start))
    outs = pl.pallas_call(
        functools.partial(
            unpack_kernel,
            groups,
            [
                (0, 0, 1, 0),
                (0, HEAD_DIM, 1, width),
                (0, PAIR, 2, 0),
                (0, PAIR + HEAD_DIM, 3, 0),
            ],
        ),
        grid=(1,),
        out_shape=[full] * 3,
        in_specs=[pl.BlockSpec(fourth.shape, lambda i: (0, 0, 0))],
        out_specs=[column(0, 2), column(0, 1), column(0, 1)],
        compiler_params=params,
        name="unpack",
    )(fourth)
    outs, sum_1 = lax.optimization_barrier((tuple(outs), sum_1))
    fifth = exchange(combine(me, groups, [dq_2], [sum_1], True), groups)
    sixth = exchange(combine(me, groups, [], [sum_2], True), groups)
    steps = len(STEPS)
    tail = pl.BlockSpec((pl.Element(block), pl.Element(2 * width)), lambda i: (0, width))
    steps = len(STEPS)
    whole = lambda piece: pl.BlockSpec(piece.shape, lambda i: (0, 0))
    return tuple(
        pl.pallas_call(
            functools.partial(
                unpack_pieces_kernel,
                groups,
                [
                    (0, 0, 0, 0),
                    (0, HEAD_DIM, 1, 0),
                    (0, PAIR, 2, 0),
                    (steps, 0, 1, width),
                    (steps, HEAD_DIM, 2, width),
                ],
                2 * steps + 3,
            ),
            grid=(1,),
            out_shape=[full] * 3,
            in_specs=[pl.BlockSpec(memory_space=pltpu.SMEM)]
            + [whole(piece) for piece in (*fifth, *sixth)]
            + [pl.BlockSpec(memory_space=pl.ANY)] * 3,
            out_specs=[column(2, 1), tail, tail],
            input_output_aliases={1 + 2 * steps + i: i for i in range(3)},
            compiler_params=params,
            name="unpack_last",
        )(me, *fifth, *sixth, *outs)
    )


def solution(mesh):
    spec = P(("frames", "heads"), None)
    return jax.shard_map(
        local, mesh=mesh, in_specs=(spec,) * 4 + (P(),), out_specs=(spec,) * 3, check_vma=False
    )
```
